32 devices in a mesh: seq: 16 (over z, y, x), blk: 2 (over core).
Axes of the slice: x: 2, y: 2, z: 4, core: 2. Of those that a mesh axis runs over, the one named last changes fastest.
Arguments:
- base_ids: int32 [8192], P('seq'), may hold values from 0 to 3
- span_start: int32 [1024], replicated, may hold values from 0 to 8184
- span_length: int32 [1024], replicated, may hold values from 1 to 8
- embedding: bfloat16 [5, 2048], P(None, 'blk'), may hold values from -6 to 6
- conv_kernel: bfloat16 [2, 9, 2048], P(None, None, 'blk'), may hold values from -2 to 2
- mix_weight: bfloat16 [2, 2048, 2048], P(None, 'blk'), may hold values from -0.125 to 0.125
- saved_input: bfloat16 [8192, 2048], P('seq', 'blk'), may hold values from -6 to 6
- cotangent: bfloat16 [8192, 2048], P('seq', 'blk'), may hold values from -6 to 6
Outputs:
- input_grad: bfloat16 [8192, 2048], P('seq', 'blk')
- weight_grad: float32 [2, 2048, 2048], P(None, ('blk', 'seq'))
- kernel_grad: float32 [2, 9, 2048], P(None, None, 'blk')
- embed_grad: float32 [5, 2048], P(None, 'blk')
The draws below stay inside these ranges and needn't reach their ends.
Inputs may be any that keep to these rules, and one draw needn't show every extreme that they name: Span j masks the positions span_start[j] to span_start[j] + span_length[j] - 1, all inside the window; spans may share positions or touch.
All inputs are finite; a program needn't handle non-finite values.
Results may differ from the reference program's by a relative error of at most 0.007.
Values may be sent and summed in bfloat16 or wider, within the bound.
A program may use at most 64 MiB of HBM per device.

```python
import math
import jax
import jax.numpy as jnp
from jax import lax

D = 2048
KSIZE = 9
BASE_DILATION = 4
NB = 2
VOCAB = 5
MAXLEN = 8
TOKENS = 8192
SPANS = 1024


def set_ends(values, rng, low, largest):
    longest = values.shape.index(max(values.shape))
    spots = []
    for shift in (0, 1):
        where = [jax.random.randint(jax.random.fold_in(rng, axis), (), 0, length) for axis, length in enumerate(values.shape)]
        where[longest] = (where[longest] + shift) % values.shape[longest]
        spots.append(tuple(where))
    return values.at[spots[0]].set(low).at[spots[1]].set(largest)


def level_of(key, dims, pieces, least, top_value):
    gain, own = 1.0, jax.random.fold_in(key, 6)
    for dim, blocks in pieces:
        draws = jnp.exp(jax.random.uniform(jax.random.fold_in(own, dim), (blocks,), jnp.float32, least / len(pieces), top_value / len(pieces)))
        gain = gain * jnp.repeat(draws, dims[dim] // blocks).reshape([-1 if axis == dim else 1 for axis in range(len(dims))])
    return gain


def noise(stream_key, dims, width, reach, pieces=(), kind=jnp.bfloat16):
    values = width * jax.random.normal(stream_key, dims, jnp.float32)
    if pieces:
        values = values * level_of(stream_key, dims, pieces, -0.22, 0.18)
    return jnp.clip(values, -reach, reach).astype(kind)


def setup_inputs(seed: int = 0) -> dict:
    key_of = jax.random.split(jax.random.key(seed), 9)
    base_ids = set_ends(jax.random.randint(key_of[0], (TOKENS,), 0, 4), jax.random.fold_in(key_of[0], 1), 0, 3).astype(jnp.int32)
    span_start = set_ends(jax.random.randint(key_of[1], (SPANS,), 0, TOKENS - MAXLEN + 1), jax.random.fold_in(key_of[1], 1), 0, TOKENS - MAXLEN).astype(jnp.int32)
    span_length = set_ends(jax.random.randint(key_of[2], (SPANS,), 1, MAXLEN + 1), jax.random.fold_in(key_of[2], 1), 1, MAXLEN).astype(jnp.int32)
    embedding = noise(key_of[3], (VOCAB, D), 1.0, 6.0, ((1, 2),))
    conv_kernel = noise(key_of[4], (NB, KSIZE, D), KSIZE ** -0.5, 2.0, ((2, 2),))
    mix_weight = noise(key_of[5], (NB, D, D), D ** -0.5, 0.125, ((1, 2),))
    saved_input = noise(key_of[6], (TOKENS, D), 1.0, 6.0, ((0, 16), (1, 2)))
    cotangent = noise(key_of[7], (TOKENS, D), 1.0, 6.0, ((0, 16), (1, 2)))
    return {"base_ids": base_ids, "span_start": span_start, "span_length": span_length, "embedding": embedding, "conv_kernel": conv_kernel, "mix_weight": mix_weight, "saved_input": saved_input, "cotangent": cotangent}


mask_token = 4
gelu_scale = 0.7978845608028654
gelu_cubic = 0.044715

def gelu_pair(pre_act):
    inner_arg = gelu_scale * (pre_act + gelu_cubic * pre_act * pre_act * pre_act)
    tangent = jnp.tanh(inner_arg)
    activation = 0.5 * pre_act * (1.0 + tangent)
    derivative = 0.5 * (1.0 + tangent) + 0.5 * pre_act * (1.0 - tangent * tangent) * gelu_scale * (1.0 + 3.0 * gelu_cubic * pre_act * pre_act)
    return (activation, derivative)

def tap_sum(padded, kernel, tap_spacing, row_count, flipped):
    tap_count = kernel.shape[0]
    running = jnp.zeros((row_count, padded.shape[1]), jnp.float32)
    for tap_index in range(tap_count):
        source = tap_count - 1 - tap_index if flipped else tap_index
        window = padded[source * tap_spacing:source * tap_spacing + row_count].astype(jnp.float32)
        running = running + kernel[tap_index].astype(jnp.float32) * window
    return running

def tap_products(grad_pre, padded, tap_spacing, tap_count):
    row_count = grad_pre.shape[0]
    grad_wide = grad_pre.astype(jnp.float32)
    output_rows = []
    for tap_index in range(tap_count):
        window = padded[tap_index * tap_spacing:tap_index * tap_spacing + row_count].astype(jnp.float32)
        output_rows.append(lax.optimization_barrier(jnp.sum(grad_wide * window, axis=0)))
    return jnp.stack(output_rows)

def reference(base_ids, span_start, span_length, embedding, conv_kernel, mix_weight, saved_input, cotangent):
    span_marks = jnp.zeros((TOKENS + 1,), jnp.int32)
    span_marks = span_marks.at[span_start].add(1).at[span_start + span_length].add(-1)
    covered = jnp.cumsum(span_marks)[:TOKENS] > 0
    masked_ids = jnp.where(covered, mask_token, base_ids).astype(jnp.int32)
    block_inputs = [embedding[masked_ids], saved_input]
    grad_scale = 1.0 / math.sqrt(TOKENS)
    upstream = jnp.where(covered[:, None], cotangent, jnp.zeros_like(cotangent))
    weight_list = [None] * NB
    kernel_list = [None] * NB
    for block_number in range(NB - 1, -1, -1):
        tap_spacing = BASE_DILATION * 2 ** block_number
        reach_rows = KSIZE // 2 * tap_spacing
        padded_in = jnp.pad(block_inputs[block_number], ((reach_rows, reach_rows), (0, 0)))
        pre_act = tap_sum(padded_in, conv_kernel[block_number], tap_spacing, TOKENS, False)
        activation, derivative = gelu_pair(pre_act)
        act_half = activation.astype(jnp.bfloat16)
        grad_act = jnp.dot(upstream, mix_weight[block_number].T, preferred_element_type=jnp.float32)
        grad_pre = (grad_act * derivative).astype(jnp.bfloat16)
        weight_list[block_number] = jnp.dot(act_half.T, upstream, preferred_element_type=jnp.float32) * grad_scale
        kernel_list[block_number] = tap_products(grad_pre, padded_in, tap_spacing, KSIZE) * grad_scale
        padded_grad = jnp.pad(grad_pre, ((reach_rows, reach_rows), (0, 0)))
        upstream = (upstream.astype(jnp.float32) + tap_sum(padded_grad, conv_kernel[block_number], tap_spacing, TOKENS, True)).astype(jnp.bfloat16)
    one_hot = (jnp.arange(VOCAB, dtype=jnp.int32)[:, None] == masked_ids[None, :]).astype(jnp.bfloat16)
    embed_grad = jnp.dot(one_hot, upstream, preferred_element_type=jnp.float32) * grad_scale
    return (upstream, jnp.stack(weight_list), jnp.stack(kernel_list), embed_grad)
```

```python
import math

import jax
import jax.numpy as jnp
from jax import lax
from jax.sharding import PartitionSpec as P

BASE_DILATION = 4


mask_token = 4
gelu_scale = 0.7978845608028654
gelu_cubic = 0.044715


def extended(cells, sides, width):
    for axis, dim in sides:
        count = lax.axis_size(axis)
        ends = count - 1
        head = lax.slice_in_dim(cells, 0, width, axis=dim)
        tail = lax.slice_in_dim(cells, cells.shape[dim] - width, cells.shape[dim], axis=dim)
        cells = jnp.concatenate(
            [
                lax.ppermute(tail, axis, [(i, (i + 1) % count) for i in range(ends)]),
                cells,
                lax.ppermute(head, axis, [((i + 1) % count, i) for i in range(ends)]),
            ],
            axis=dim,
        )
    return cells


def gelu_pair(pre_act):
    inner_arg = gelu_scale * (pre_act + gelu_cubic * pre_act * pre_act * pre_act)
    tangent = jnp.tanh(inner_arg)
    activation = 0.5 * pre_act * (1.0 + tangent)
    derivative = 0.5 * (1.0 + tangent) + 0.5 * pre_act * (1.0 - tangent * tangent) * gelu_scale * (
        1.0 + 3.0 * gelu_cubic * pre_act * pre_act
    )
    return (activation, derivative)


def tap_sum(padded, kernel, tap_spacing, row_count, flipped):
    tap_count = kernel.shape[0]
    running = jnp.zeros((row_count, padded.shape[1]), jnp.float32)
    for tap_index in range(tap_count):
        source = tap_count - 1 - tap_index if flipped else tap_index
        window = padded[source * tap_spacing : source * tap_spacing + row_count].astype(jnp.float32)
        running = running + kernel[tap_index].astype(jnp.float32) * window
    return running


def tap_products(grad_pre, padded, tap_spacing, tap_count):
    row_count = grad_pre.shape[0]
    grad_wide = grad_pre.astype(jnp.float32)
    output_rows = []
    for tap_index in range(tap_count):
        window = padded[tap_index * tap_spacing : tap_index * tap_spacing + row_count].astype(
            jnp.float32
        )
        output_rows.append(jnp.sum(grad_wide * window, axis=0))
    return jnp.stack(output_rows)


def covered_at(positions, span_start, span_length):
    span_end = span_start + span_length
    within = (positions[:, None] >= span_start[None, :]) & (positions[:, None] < span_end[None, :])
    return jnp.any(within, axis=1)


def lookup(hot_rows, table_rows):
    return jnp.einsum("vt,vc->tc", hot_rows, table_rows, preferred_element_type=jnp.float32).astype(
        jnp.bfloat16
    )


def exchanged(cells, axis, bit):
    count = lax.axis_size(axis)
    return lax.ppermute(cells, axis, [(i, i ^ (1 << bit)) for i in range(count)])


def halved_sum(part, order):
    bits = len(order)
    me = lax.axis_index("seq")
    part = part.reshape((2,) * bits + (part.shape[0] >> bits, part.shape[1]))
    axes = list(range(bits - 1, -1, -1))
    for step, bit in enumerate(order):
        dim = axes.index(bit)
        mine = (me >> bit) & 1
        send = lax.dynamic_index_in_dim(part, 1 - mine, dim, keepdims=False)
        keep = lax.dynamic_index_in_dim(part, mine, dim, keepdims=False)
        axes.remove(bit)
        total = keep.astype(jnp.float32) + exchanged(send, "seq", bit).astype(jnp.float32)
        part = total if step == bits - 1 else total.astype(jnp.bfloat16)
    return part


def doubled_sum(part, order):
    for bit in order:
        part = part + exchanged(part, "seq", bit)
    return part


def on_device(
    base_ids, span_start, span_length, embedding, conv_kernel, mix_weight, saved_input, cotangent
):
    row_count = saved_input.shape[0]
    block_count = conv_kernel.shape[0]
    tap_count = conv_kernel.shape[1]
    taps_per_side = tap_count // 2
    vocab_rows = embedding.shape[0]
    total_rows = row_count * lax.axis_size("seq")
    grad_scale = 1.0 / math.sqrt(total_rows)
    first_row = lax.axis_index("seq") * row_count
    positions = first_row + jnp.arange(row_count, dtype=jnp.int32)
    covered = covered_at(positions, span_start, span_length)
    masked_ids = jnp.where(covered, mask_token, base_ids)
    vocab_ids = jnp.arange(vocab_rows, dtype=jnp.int32)
    one_hot = (vocab_ids[:, None] == masked_ids[None, :]).astype(jnp.bfloat16)
    bits = (lax.axis_size("seq") - 1).bit_length()
    orders = (tuple(range(bits)), (1, 0) + tuple(range(2, bits)))
    initial_reach = taps_per_side * BASE_DILATION
    first_input = lookup(one_hot, embedding)
    first_padded = extended(first_input, (("seq", 0),), initial_reach)
    upstream = jnp.where(covered[:, None], cotangent, jnp.zeros_like(cotangent))
    weight_parts = [None] * block_count
    kernel_parts = [None] * block_count
    for block_number in range(block_count - 1, -1, -1):
        tap_spacing = BASE_DILATION * 2**block_number
        reach_rows = taps_per_side * tap_spacing
        if block_number == 0:
            padded_in = first_padded
        else:
            padded_in = extended(saved_input, (("seq", 0),), reach_rows)
        kernel = conv_kernel[block_number]
        weight_rows = mix_weight[block_number]
        pre_act = tap_sum(padded_in, kernel, tap_spacing, row_count, False)
        activation, derivative = gelu_pair(pre_act)
        act_half = activation.astype(jnp.bfloat16)
        column_piece = lax.all_gather(upstream, "blk", axis=1, tiled=True)
        grad_held = lax.dot_general(
            column_piece, weight_rows, (((1,), (1,)), ((), ())), preferred_element_type=jnp.float32
        )
        halves = []
        for chunk, order in enumerate(orders):
            width = column_piece.shape[1] // len(orders)
            part = lax.dot_general(
                act_half,
                lax.slice_in_dim(column_piece, chunk * width, (chunk + 1) * width, axis=1),
                (((0,), (0,)), ((), ())),
                preferred_element_type=jnp.float32,
            ).astype(jnp.bfloat16)
            halves.append(halved_sum(part, order))
        grad_pre = (grad_held * derivative).astype(jnp.bfloat16)
        kernel_parts[block_number] = (
            tap_products(grad_pre, padded_in, tap_spacing, tap_count) * grad_scale
        )
        padded_grad = extended(grad_pre, (("seq", 0),), reach_rows)
        upstream = (
            upstream.astype(jnp.float32)
            + tap_sum(padded_grad, kernel, tap_spacing, row_count, True)
        ).astype(jnp.bfloat16)
        weight_parts[block_number] = jnp.concatenate(halves, axis=1) * grad_scale
    weight_grad = jnp.stack(weight_parts)
    embed_part = jnp.dot(one_hot, upstream, preferred_element_type=jnp.float32) * grad_scale
    sums = [doubled_sum(part, orders[0]) for part in kernel_parts[1:]]
    last = doubled_sum(jnp.concatenate([kernel_parts[0], embed_part]), orders[1])
    kernel_grad = jnp.stack([last[:tap_count]] + sums)
    embed_grad = last[tap_count:]
    return (upstream, weight_grad, kernel_grad, embed_grad)


def solution(mesh):
    placed = (
        P("seq"),
        P(),
        P(),
        P(None, "blk"),
        P(None, None, "blk"),
        P(None, "blk", None),
        P("seq", "blk"),
        P("seq", "blk"),
    )
    return jax.shard_map(
        on_device,
        mesh=mesh,
        in_specs=placed,
        out_specs=(
            P("seq", "blk"),
            P(None, ("blk", "seq"), None),
            P(None, None, "blk"),
            P(None, "blk"),
        ),
        check_vma=False,
    )
```

```python
import math

import jax
import jax.numpy as jnp
from jax import lax
from jax.sharding import PartitionSpec as P

BASE_DILATION = 4


mask_token = 4
gelu_scale = 0.7978845608028654
gelu_cubic = 0.044715


def extended(cells, sides, width):
    for axis, dim in sides:
        count = lax.axis_size(axis)
        ends = count - 1
        head = lax.slice_in_dim(cells, 0, width, axis=dim)
        tail = lax.slice_in_dim(cells, cells.shape[dim] - width, cells.shape[dim], axis=dim)
        cells = jnp.concatenate(
            [
                lax.ppermute(tail, axis, [(i, (i + 1) % count) for i in range(ends)]),
                cells,
                lax.ppermute(head, axis, [((i + 1) % count, i) for i in range(ends)]),
            ],
            axis=dim,
        )
    return cells


def padded_together(arrays, widths):
    count = lax.axis_size("seq")
    ends = count - 1
    heads = jnp.concatenate([cells[:width] for cells, width in zip(arrays, widths)])
    tails = jnp.concatenate([cells[-width:] for cells, width in zip(arrays, widths)])
    before = lax.ppermute(tails, "seq", [(i, (i + 1) % count) for i in range(ends)])
    after = lax.ppermute(heads, "seq", [((i + 1) % count, i) for i in range(ends)])
    padded, first = [], 0
    for cells, width in zip(arrays, widths):
        rows = slice(first, first + width)
        padded.append(jnp.concatenate([before[rows], cells, after[rows]]))
        first += width
    return padded


def gelu_pair(pre_act):
    inner_arg = gelu_scale * (pre_act + gelu_cubic * pre_act * pre_act * pre_act)
    tangent = jnp.tanh(inner_arg)
    activation = 0.5 * pre_act * (1.0 + tangent)
    derivative = 0.5 * (1.0 + tangent) + 0.5 * pre_act * (1.0 - tangent * tangent) * gelu_scale * (
        1.0 + 3.0 * gelu_cubic * pre_act * pre_act
    )
    return (activation, derivative)


def tap_sum(padded, kernel, tap_spacing, row_count, flipped):
    tap_count = kernel.shape[0]
    running = jnp.zeros((row_count, padded.shape[1]), jnp.float32)
    for tap_index in range(tap_count):
        source = tap_count - 1 - tap_index if flipped else tap_index
        window = padded[source * tap_spacing : source * tap_spacing + row_count].astype(jnp.float32)
        running = running + kernel[tap_index].astype(jnp.float32) * window
    return running


def tap_products(grad_pre, padded, tap_spacing, tap_count):
    row_count = grad_pre.shape[0]
    grad_wide = grad_pre.astype(jnp.float32)
    output_rows = []
    for tap_index in range(tap_count):
        window = padded[tap_index * tap_spacing : tap_index * tap_spacing + row_count].astype(
            jnp.float32
        )
        output_rows.append(jnp.sum(grad_wide * window, axis=0))
    return jnp.stack(output_rows)


def covered_at(positions, span_start, span_length):
    span_end = span_start + span_length
    within = (positions[:, None] >= span_start[None, :]) & (positions[:, None] < span_end[None, :])
    return jnp.any(within, axis=1)


def lookup(hot_rows, table_rows):
    return jnp.einsum("vt,vc->tc", hot_rows, table_rows, preferred_element_type=jnp.float32).astype(
        jnp.bfloat16
    )


def exchanged(cells, axis, bit):
    count = lax.axis_size(axis)
    return lax.ppermute(cells, axis, [(i, i ^ (1 << bit)) for i in range(count)])


def split_rows(part, bits):
    return part.reshape((2,) * bits + (part.shape[0] >> bits, part.shape[1]))


def halving_step(part, order, step):
    bit = order[step]
    dim = sorted(order[step:], reverse=True).index(bit)
    mine = (lax.axis_index("seq") >> bit) & 1
    send = lax.dynamic_index_in_dim(part, 1 - mine, dim, keepdims=False)
    keep = lax.dynamic_index_in_dim(part, mine, dim, keepdims=False)
    return (keep, exchanged(send, "seq", bit))


def added(keep, arrived, last):
    total = keep.astype(jnp.float32) + arrived.astype(jnp.float32)
    return total if last else total.astype(jnp.bfloat16)


def halving_steps(parts, orders, steps):
    pairs = None
    for step in steps:
        if pairs is not None:
            parts = [added(keep, arrived, False) for keep, arrived in pairs]
        pairs = [halving_step(part, order, step) for part, order in zip(parts, orders)]
    return pairs


def finished(pairs, scale):
    return jnp.concatenate([added(keep, arrived, True) for keep, arrived in pairs], axis=1) * scale


def tied(value, pairs):
    value, pairs = lax.optimization_barrier((value, pairs))
    return (value, pairs)


def doubled_sum(part, order):
    for bit in order:
        part = part + exchanged(part, "seq", bit)
    return part


def on_device(
    base_ids, span_start, span_length, embedding, conv_kernel, mix_weight, saved_input, cotangent
):
    row_count = saved_input.shape[0]
    block_count = conv_kernel.shape[0]
    tap_count = conv_kernel.shape[1]
    taps_per_side = tap_count // 2
    vocab_rows = embedding.shape[0]
    total_rows = row_count * lax.axis_size("seq")
    grad_scale = 1.0 / math.sqrt(total_rows)
    first_row = lax.axis_index("seq") * row_count
    positions = first_row + jnp.arange(row_count, dtype=jnp.int32)
    covered = covered_at(positions, span_start, span_length)
    masked_ids = jnp.where(covered, mask_token, base_ids)
    vocab_ids = jnp.arange(vocab_rows, dtype=jnp.int32)
    one_hot = (vocab_ids[:, None] == masked_ids[None, :]).astype(jnp.bfloat16)
    bits = (lax.axis_size("seq") - 1).bit_length()
    orders = (tuple(range(bits)), (1, 0) + tuple(range(2, bits)))
    first_input = lookup(one_hot, embedding)
    steps = len(orders[0])
    halo_rows = [taps_per_side * BASE_DILATION * 2**number for number in range(block_count)]
    padded_inputs = padded_together((first_input, saved_input), halo_rows)
    upstream = jnp.where(covered[:, None], cotangent, jnp.zeros_like(cotangent))
    weight_parts = [None] * block_count
    kernel_parts = [None] * block_count
    earlier = None
    for block_number in range(block_count - 1, -1, -1):
        tap_spacing = BASE_DILATION * 2**block_number
        padded_in = padded_inputs[block_number]
        kernel = conv_kernel[block_number]
        column_piece = lax.all_gather(upstream, "blk", axis=1, tiled=True)
        pre_act = tap_sum(padded_in, kernel, tap_spacing, row_count, False)
        activation, derivative = gelu_pair(pre_act)
        act_half = activation.astype(jnp.bfloat16)
        if earlier is not None:
            parts = [added(keep, arrived, False) for keep, arrived in earlier]
            pairs = halving_steps(parts, orders, range(1, 2))
            column_piece, earlier = tied(column_piece, pairs)
        width = column_piece.shape[1] // len(orders)
        parts = [
            lax.dot_general(
                act_half,
                lax.slice_in_dim(column_piece, chunk * width, (chunk + 1) * width, axis=1),
                (((0,), (0,)), ((), ())),
                preferred_element_type=jnp.float32,
            ).astype(jnp.bfloat16)
            for chunk in range(len(orders))
        ]
        column_piece, parts = lax.optimization_barrier((column_piece, parts))
        parts = [split_rows(part, steps) for part in parts]
        pairs = halving_steps(parts, orders, range(0, 1))
        if earlier is not None:
            parts = [added(keep, arrived, False) for keep, arrived in earlier]
            earlier = halving_steps(parts, orders, range(2, 3))
        grad_held = lax.dot_general(
            column_piece,
            mix_weight[block_number],
            (((1,), (1,)), ((), ())),
            preferred_element_type=jnp.float32,
        )
        grad_pre = (grad_held * derivative).astype(jnp.bfloat16)
        if earlier is not None:
            grad_pre, earlier = tied(grad_pre, earlier)
            parts = [added(keep, arrived, False) for keep, arrived in earlier]
            earlier = halving_steps(parts, orders, range(3, steps))
        kernel_parts[block_number] = (
            tap_products(grad_pre, padded_in, tap_spacing, tap_count) * grad_scale
        )
        padded_grad = extended(grad_pre, (("seq", 0),), halo_rows[block_number])
        upstream = (
            upstream.astype(jnp.float32)
            + tap_sum(padded_grad, kernel, tap_spacing, row_count, True)
        ).astype(jnp.bfloat16)
        if block_number > 0:
            upstream, earlier = tied(upstream, pairs)
        else:
            upstream, (earlier, pairs) = tied(upstream, (earlier, pairs))
            weight_parts[1] = finished(earlier, grad_scale)
            parts = [added(keep, arrived, False) for keep, arrived in pairs]
            weight_parts[0] = finished(halving_steps(parts, orders, range(1, steps)), grad_scale)
    weight_grad = jnp.stack(weight_parts)
    embed_part = jnp.dot(one_hot, upstream, preferred_element_type=jnp.float32) * grad_scale
    sums = doubled_sum(jnp.concatenate(kernel_parts + [embed_part]), orders[0])
    kernel_grad = sums[: block_count * tap_count].reshape(block_count, tap_count, -1)
    embed_grad = sums[block_count * tap_count :]
    return (upstream, weight_grad, kernel_grad, embed_grad)


def solution(mesh):
    placed = (
        P("seq"),
        P(),
        P(),
        P(None, "blk"),
        P(None, None, "blk"),
        P(None, "blk", None),
        P("seq", "blk"),
        P("seq", "blk"),
    )
    return jax.shard_map(
        on_device,
        mesh=mesh,
        in_specs=placed,
        out_specs=(
            P("seq", "blk"),
            P(None, ("blk", "seq"), None),
            P(None, None, "blk"),
            P(None, "blk"),
        ),
        check_vma=False,
    )
```

```python
import math

import jax
import jax.numpy as jnp
from jax import lax
from jax.sharding import PartitionSpec as P

BASE_DILATION = 4


mask_token = 4
gelu_scale = 0.7978845608028654
gelu_cubic = 0.044715


def edge_rows(cells, width):
    count = lax.axis_size("seq")
    ends = count - 1
    return (
        lax.ppermute(cells[-width:], "seq", [(i, (i + 1) % count) for i in range(ends)]),
        lax.ppermute(cells[:width], "seq", [((i + 1) % count, i) for i in range(ends)]),
    )


def padded_together(arrays, widths):
    count = lax.axis_size("seq")
    ends = count - 1
    heads = jnp.concatenate([cells[:width] for cells, width in zip(arrays, widths)])
    tails = jnp.concatenate([cells[-width:] for cells, width in zip(arrays, widths)])
    before = lax.ppermute(tails, "seq", [(i, (i + 1) % count) for i in range(ends)])
    after = lax.ppermute(heads, "seq", [((i + 1) % count, i) for i in range(ends)])
    padded, first = [], 0
    for cells, width in zip(arrays, widths):
        rows = slice(first, first + width)
        padded.append(jnp.concatenate([before[rows], cells, after[rows]]))
        first += width
    return padded


def gelu_pair(pre_act):
    inner_arg = gelu_scale * (pre_act + gelu_cubic * pre_act * pre_act * pre_act)
    tangent = jnp.tanh(inner_arg)
    activation = 0.5 * pre_act * (1.0 + tangent)
    derivative = 0.5 * (1.0 + tangent) + 0.5 * pre_act * (1.0 - tangent * tangent) * gelu_scale * (
        1.0 + 3.0 * gelu_cubic * pre_act * pre_act
    )
    return (activation, derivative)


def tap_sum(padded, kernel, tap_spacing, row_count, flipped):
    tap_count = kernel.shape[0]
    running = jnp.zeros((row_count, padded.shape[1]), jnp.float32)
    for tap_index in range(tap_count):
        source = tap_count - 1 - tap_index if flipped else tap_index
        window = padded[source * tap_spacing : source * tap_spacing + row_count].astype(jnp.float32)
        running = running + kernel[tap_index].astype(jnp.float32) * window
    return running


def tap_products(grad_pre, padded, tap_spacing, tap_count):
    row_count = grad_pre.shape[0]
    grad_wide = grad_pre.astype(jnp.float32)
    output_rows = []
    for tap_index in range(tap_count):
        window = padded[tap_index * tap_spacing : tap_index * tap_spacing + row_count].astype(
            jnp.float32
        )
        output_rows.append(jnp.sum(grad_wide * window, axis=0))
    return jnp.stack(output_rows)


def covered_at(positions, span_start, span_length):
    span_end = span_start + span_length
    within = (positions[:, None] >= span_start[None, :]) & (positions[:, None] < span_end[None, :])
    return jnp.any(within, axis=1)


def lookup(hot_rows, table_rows):
    return jnp.einsum("vt,vc->tc", hot_rows, table_rows, preferred_element_type=jnp.float32).astype(
        jnp.bfloat16
    )


def exchanged(cells, axis, bit):
    count = lax.axis_size(axis)
    return lax.ppermute(cells, axis, [(i, i ^ (1 << bit)) for i in range(count)])


def split_rows(part, bits):
    return part.reshape((2,) * bits + (part.shape[0] >> bits, part.shape[1]))


def halves_of(parts, orders, step):
    halves = []
    for part, order in zip(parts, orders):
        bit = order[step]
        dim = sorted(order[step:], reverse=True).index(bit)
        mine = (lax.axis_index("seq") >> bit) & 1
        send = lax.dynamic_index_in_dim(part, 1 - mine, dim, keepdims=False)
        keep = lax.dynamic_index_in_dim(part, mine, dim, keepdims=False)
        halves.append((keep, send))
    return halves


def swapped(halves, orders, step):
    return [
        (keep, exchanged(send, "seq", order[step])) for (keep, send), order in zip(halves, orders)
    ]


def added(keep, arrived, last):
    total = keep.astype(jnp.float32) + arrived.astype(jnp.float32)
    return total if last else total.astype(jnp.bfloat16)


def next_halves(pairs, orders, step):
    return halves_of([added(keep, arrived, False) for keep, arrived in pairs], orders, step)


def kept_with(value, pairs):
    kept = [keep for keep, arrived in pairs]
    value, kept = lax.optimization_barrier((value, kept))
    return (value, [(keep, arrived) for keep, (_, arrived) in zip(kept, pairs)])


def later_steps(pairs, orders, steps):
    for step in steps:
        pairs = swapped(next_halves(pairs, orders, step), orders, step)
    return pairs


def finished(pairs, scale):
    return jnp.concatenate([added(keep, arrived, True) for keep, arrived in pairs], axis=1) * scale


def on_device(
    base_ids, span_start, span_length, embedding, conv_kernel, mix_weight, saved_input, cotangent
):
    row_count = saved_input.shape[0]
    block_count = conv_kernel.shape[0]
    tap_count = conv_kernel.shape[1]
    taps_per_side = tap_count // 2
    vocab_rows = embedding.shape[0]
    total_rows = row_count * lax.axis_size("seq")
    grad_scale = 1.0 / math.sqrt(total_rows)
    first_row = lax.axis_index("seq") * row_count
    positions = first_row + jnp.arange(row_count, dtype=jnp.int32)
    covered = covered_at(positions, span_start, span_length)
    masked_ids = jnp.where(covered, mask_token, base_ids)
    vocab_ids = jnp.arange(vocab_rows, dtype=jnp.int32)
    one_hot = (vocab_ids[:, None] == masked_ids[None, :]).astype(jnp.bfloat16)
    bits = (lax.axis_size("seq") - 1).bit_length()
    orders = (tuple(range(bits)), (1, 0) + tuple(range(2, bits)))
    first_input = lookup(one_hot, embedding)
    steps = len(orders[0])
    halo_rows = [taps_per_side * BASE_DILATION * 2**number for number in range(block_count)]
    padded_inputs = padded_together((first_input, saved_input), halo_rows)
    upstream = jnp.where(covered[:, None], cotangent, jnp.zeros_like(cotangent))
    kernel_parts = [None] * block_count
    earlier = None
    for block_number in range(block_count - 1, -1, -1):
        tap_spacing = BASE_DILATION * 2**block_number
        reach_rows = halo_rows[block_number]
        padded_in = padded_inputs[block_number]
        kernel = conv_kernel[block_number]
        column_piece = lax.all_gather(upstream, "blk", axis=1, tiled=True)
        if earlier is not None:
            padded_in, earlier = lax.optimization_barrier((padded_in, earlier))
        pre_act = tap_sum(padded_in, kernel, tap_spacing, row_count, False)
        activation, derivative = gelu_pair(pre_act)
        act_half = activation.astype(jnp.bfloat16)
        if earlier is not None:
            halves = next_halves(earlier, orders, 1)
            earlier = swapped(halves, orders, 1)
            column_piece, earlier = kept_with(column_piece, earlier)
        grad_held = lax.dot_general(
            column_piece,
            mix_weight[block_number],
            (((1,), (1,)), ((), ())),
            preferred_element_type=jnp.float32,
        )
        grad_pre = (grad_held * derivative).astype(jnp.bfloat16)
        edges = edge_rows(grad_pre, reach_rows)
        act_half, grad_pre = lax.optimization_barrier((act_half, grad_pre))
        width = column_piece.shape[1] // len(orders)
        parts = [
            split_rows(
                lax.dot_general(
                    act_half,
                    lax.slice_in_dim(column_piece, chunk * width, (chunk + 1) * width, axis=1),
                    (((0,), (0,)), ((), ())),
                    preferred_element_type=jnp.float32,
                ).astype(jnp.bfloat16),
                steps,
            )
            for chunk in range(len(orders))
        ]
        halves = halves_of(parts, orders, 0)
        pairs = swapped(halves, orders, 0)
        edges, pairs = kept_with(edges, pairs)
        if earlier is not None:
            edges, earlier = lax.optimization_barrier((edges, earlier))
        if earlier is not None:
            earlier = later_steps(earlier, orders, range(2, 3))
        kernel_parts[block_number] = (
            tap_products(grad_pre, padded_in, tap_spacing, tap_count) * grad_scale
        )
        padded_grad = jnp.concatenate([edges[0], grad_pre, edges[1]])
        upstream = (
            upstream.astype(jnp.float32)
            + tap_sum(padded_grad, kernel, tap_spacing, row_count, True)
        ).astype(jnp.bfloat16)
        if block_number > 0:
            earlier = pairs
    embed_part = jnp.dot(one_hot, upstream, preferred_element_type=jnp.float32) * grad_scale
    sums = jnp.concatenate(kernel_parts + [embed_part])
    for step in range(steps):
        sums = sums + exchanged(sums, "seq", steps - 1 - step)
        if step == 0:
            sums, earlier = lax.optimization_barrier((sums, earlier))
            earlier = later_steps(earlier, orders, range(3, steps))
        elif step < 4:
            sums, pairs, earlier = lax.optimization_barrier((sums, pairs, earlier))
            pairs = later_steps(pairs, orders, range(step, step + 1 if step < 3 else steps))
    weight_parts = [finished(pairs, grad_scale), finished(earlier, grad_scale)]
    weight_grad = jnp.stack(weight_parts)
    kernel_grad = sums[: block_count * tap_count].reshape(block_count, tap_count, -1)
    embed_grad = sums[block_count * tap_count :]
    return (upstream, weight_grad, kernel_grad, embed_grad)


def solution(mesh):
    placed = (
        P("seq"),
        P(),
        P(),
        P(None, "blk"),
        P(None, None, "blk"),
        P(None, "blk", None),
        P("seq", "blk"),
        P("seq", "blk"),
    )
    return jax.shard_map(
        on_device,
        mesh=mesh,
        in_specs=placed,
        out_specs=(
            P("seq", "blk"),
            P(None, ("blk", "seq"), None),
            P(None, None, "blk"),
            P(None, "blk"),
        ),
        check_vma=False,
    )
```

```python
import math

import jax
import jax.numpy as jnp
from jax import lax
from jax.sharding import PartitionSpec as P

BASE_DILATION = 4


mask_token = 4
gelu_scale = 0.7978845608028654
gelu_cubic = 0.044715


def edge_rows(cells, width):
    count = lax.axis_size("seq")
    ends = count - 1
    return (
        lax.ppermute(cells[-width:], "seq", [(i, (i + 1) % count) for i in range(ends)]),
        lax.ppermute(cells[:width], "seq", [((i + 1) % count, i) for i in range(ends)]),
    )


def padded_together(arrays, widths):
    count = lax.axis_size("seq")
    ends = count - 1
    heads = jnp.concatenate([cells[:width] for cells, width in zip(arrays, widths)])
    tails = jnp.concatenate([cells[-width:] for cells, width in zip(arrays, widths)])
    before = lax.ppermute(tails, "seq", [(i, (i + 1) % count) for i in range(ends)])
    after = lax.ppermute(heads, "seq", [((i + 1) % count, i) for i in range(ends)])
    padded, first = [], 0
    for cells, width in zip(arrays, widths):
        rows = slice(first, first + width)
        padded.append(jnp.concatenate([before[rows], cells, after[rows]]))
        first += width
    return padded


def gelu_pair(pre_act):
    inner_arg = gelu_scale * (pre_act + gelu_cubic * pre_act * pre_act * pre_act)
    tangent = jnp.tanh(inner_arg)
    activation = 0.5 * pre_act * (1.0 + tangent)
    derivative = 0.5 * (1.0 + tangent) + 0.5 * pre_act * (1.0 - tangent * tangent) * gelu_scale * (
        1.0 + 3.0 * gelu_cubic * pre_act * pre_act
    )
    return (activation, derivative)


def tap_sum(padded, kernel, tap_spacing, row_count, flipped):
    tap_count = kernel.shape[0]
    running = jnp.zeros((row_count, padded.shape[1]), jnp.float32)
    for tap_index in range(tap_count):
        source = tap_count - 1 - tap_index if flipped else tap_index
        window = padded[source * tap_spacing : source * tap_spacing + row_count].astype(jnp.float32)
        running = running + kernel[tap_index].astype(jnp.float32) * window
    return running


def tap_products(grad_pre, padded, tap_spacing, tap_count):
    row_count = grad_pre.shape[0]
    grad_wide = grad_pre.astype(jnp.float32)
    output_rows = []
    for tap_index in range(tap_count):
        window = padded[tap_index * tap_spacing : tap_index * tap_spacing + row_count].astype(
            jnp.float32
        )
        output_rows.append(jnp.sum(grad_wide * window, axis=0))
    return jnp.stack(output_rows)


def covered_at(positions, span_start, span_length):
    span_end = span_start + span_length
    within = (positions[:, None] >= span_start[None, :]) & (positions[:, None] < span_end[None, :])
    return jnp.any(within, axis=1)


def lookup(hot_rows, table_rows):
    return jnp.einsum("vt,vc->tc", hot_rows, table_rows, preferred_element_type=jnp.float32).astype(
        jnp.bfloat16
    )


def exchanged(cells, axis, bit):
    count = lax.axis_size(axis)
    return lax.ppermute(cells, axis, [(i, i ^ (1 << bit)) for i in range(count)])


def split_rows(part, bits):
    return part.reshape((2,) * bits + (part.shape[0] >> bits, part.shape[1]))


def halves_of(arrays, order, step):
    bit = order[step]
    dim = sorted(order[step:], reverse=True).index(bit)
    mine = (lax.axis_index("seq") >> bit) & 1
    halves = []
    for index in (mine, 1 - mine):
        cut = [lax.dynamic_index_in_dim(cells, index, dim, keepdims=False) for cells in arrays]
        halves.append(cut[0] if len(cut) == 1 else added(*cut, False))
    return tuple(halves)


def swapped(halves, orders, step):
    return [
        (keep, exchanged(send, "seq", order[step])) for (keep, send), order in zip(halves, orders)
    ]


def added(keep, arrived, last):
    total = keep.astype(jnp.float32) + arrived.astype(jnp.float32)
    return total if last else total.astype(jnp.bfloat16)


def later_steps(pairs, orders, steps):
    for step in steps:
        halves = [halves_of(pair, order, step) for pair, order in zip(pairs, orders)]
        pairs = swapped(halves, orders, step)
    return pairs


def finished(pairs, scale):
    return jnp.concatenate([added(keep, arrived, True) for keep, arrived in pairs], axis=1) * scale


def on_device(
    base_ids, span_start, span_length, embedding, conv_kernel, mix_weight, saved_input, cotangent
):
    row_count = saved_input.shape[0]
    block_count = conv_kernel.shape[0]
    tap_count = conv_kernel.shape[1]
    taps_per_side = tap_count // 2
    vocab_rows = embedding.shape[0]
    total_rows = row_count * lax.axis_size("seq")
    grad_scale = 1.0 / math.sqrt(total_rows)
    first_row = lax.axis_index("seq") * row_count
    positions = first_row + jnp.arange(row_count, dtype=jnp.int32)
    covered = covered_at(positions, span_start, span_length)
    masked_ids = jnp.where(covered, mask_token, base_ids)
    vocab_ids = jnp.arange(vocab_rows, dtype=jnp.int32)
    one_hot = (vocab_ids[:, None] == masked_ids[None, :]).astype(jnp.bfloat16)
    bits = (lax.axis_size("seq") - 1).bit_length()
    orders = (tuple(range(bits)), (1, 0) + tuple(range(2, bits)))
    first_input = lookup(one_hot, embedding)
    steps = len(orders[0])
    halo_rows = [taps_per_side * BASE_DILATION * 2**number for number in range(block_count)]
    padded_inputs = padded_together((first_input, saved_input), halo_rows)
    upstream = jnp.where(covered[:, None], cotangent, jnp.zeros_like(cotangent))
    kernel_parts = [None] * block_count
    earlier = None
    for block_number in range(block_count - 1, -1, -1):
        tap_spacing = BASE_DILATION * 2**block_number
        reach_rows = halo_rows[block_number]
        padded_in = padded_inputs[block_number]
        kernel = conv_kernel[block_number]
        column_piece = lax.all_gather(upstream, "blk", axis=1, tiled=True)
        pre_act = tap_sum(padded_in, kernel, tap_spacing, row_count, False)
        activation, derivative = gelu_pair(pre_act)
        act_half = activation.astype(jnp.bfloat16)
        if earlier is not None:
            column_piece, earlier = lax.optimization_barrier((column_piece, earlier))
        grad_held = lax.dot_general(
            column_piece,
            mix_weight[block_number],
            (((1,), (1,)), ((), ())),
            preferred_element_type=jnp.float32,
        )
        grad_pre = (grad_held * derivative).astype(jnp.bfloat16)
        edges = edge_rows(grad_pre, reach_rows)
        if earlier is None:
            act_half, grad_pre = lax.optimization_barrier((act_half, grad_pre))
        else:
            act_half, grad_pre, earlier = lax.optimization_barrier((act_half, grad_pre, earlier))
            earlier = later_steps(earlier, orders, range(1, 2))
        width = column_piece.shape[1] // len(orders)
        parts = [
            split_rows(
                lax.dot_general(
                    act_half,
                    lax.slice_in_dim(column_piece, chunk * width, (chunk + 1) * width, axis=1),
                    (((0,), (0,)), ((), ())),
                    preferred_element_type=jnp.float32,
                ).astype(jnp.bfloat16),
                steps,
            )
            for chunk in range(len(orders))
        ]
        edges, parts = lax.optimization_barrier((edges, parts))
        pairs = swapped([halves_of([part], order, 0) for part, order in zip(parts, orders)], orders, 0)
        kept, edges = lax.optimization_barrier(([keep for keep, _ in pairs], edges))
        pairs = [(keep, arrived) for keep, (_, arrived) in zip(kept, pairs)]
        kernel_parts[block_number] = (
            tap_products(grad_pre, padded_in, tap_spacing, tap_count) * grad_scale
        )
        padded_grad = jnp.concatenate([edges[0], grad_pre, edges[1]])
        upstream = (
            upstream.astype(jnp.float32)
            + tap_sum(padded_grad, kernel, tap_spacing, row_count, True)
        ).astype(jnp.bfloat16)
        if block_number > 0:
            earlier = pairs
    embed_part = jnp.dot(one_hot, upstream, preferred_element_type=jnp.float32) * grad_scale
    sums = jnp.concatenate(kernel_parts + [embed_part])
    sums, pairs, earlier = lax.optimization_barrier((sums, pairs, earlier))
    earlier = later_steps(earlier, orders, range(2, 3))
    pairs = later_steps(pairs, orders, range(1, 2))
    for step in range(steps):
        sums = sums + exchanged(sums, "seq", steps - 1 - step)
        if step < 2:
            sums, pairs, earlier = lax.optimization_barrier((sums, pairs, earlier))
            pairs = later_steps(pairs, orders, range(2, 3) if step == 0 else range(3, steps))
            earlier = later_steps(earlier, orders, range(3, steps) if step == 0 else ())
    weight_parts = [finished(pairs, grad_scale), finished(earlier, grad_scale)]
    weight_grad = jnp.stack(weight_parts)
    kernel_grad = sums[: block_count * tap_count].reshape(block_count, tap_count, -1)
    embed_grad = sums[block_count * tap_count :]
    return (upstream, weight_grad, kernel_grad, embed_grad)


def solution(mesh):
    placed = (
        P("seq"),
        P(),
        P(),
        P(None, "blk"),
        P(None, None, "blk"),
        P(None, "blk", None),
        P("seq", "blk"),
        P("seq", "blk"),
    )
    return jax.shard_map(
        on_device,
        mesh=mesh,
        in_specs=placed,
        out_specs=(
            P("seq", "blk"),
            P(None, ("blk", "seq"), None),
            P(None, None, "blk"),
            P(None, "blk"),
        ),
        check_vma=False,
    )
```

```python
import math

import jax
import jax.numpy as jnp
from jax import lax
from jax.sharding import PartitionSpec as P

BASE_DILATION = 4


mask_token = 4
gelu_scale = 0.7978845608028654
gelu_cubic = 0.044715


def edge_rows(cells, width):
    count = lax.axis_size("seq")
    ends = count - 1
    return (
        lax.ppermute(cells[-width:], "seq", [(i, (i + 1) % count) for i in range(ends)]),
        lax.ppermute(cells[:width], "seq", [((i + 1) % count, i) for i in range(ends)]),
    )


def padded_together(arrays, widths):
    count = lax.axis_size("seq")
    ends = count - 1
    heads = jnp.concatenate([cells[:width] for cells, width in zip(arrays, widths)])
    tails = jnp.concatenate([cells[-width:] for cells, width in zip(arrays, widths)])
    before = lax.ppermute(tails, "seq", [(i, (i + 1) % count) for i in range(ends)])
    after = lax.ppermute(heads, "seq", [((i + 1) % count, i) for i in range(ends)])
    padded, first = [], 0
    for cells, width in zip(arrays, widths):
        rows = slice(first, first + width)
        padded.append(jnp.concatenate([before[rows], cells, after[rows]]))
        first += width
    return padded


def gelu_pair(pre_act):
    inner_arg = gelu_scale * (pre_act + gelu_cubic * pre_act * pre_act * pre_act)
    tangent = jnp.tanh(inner_arg)
    activation = 0.5 * pre_act * (1.0 + tangent)
    derivative = 0.5 * (1.0 + tangent) + 0.5 * pre_act * (1.0 - tangent * tangent) * gelu_scale * (
        1.0 + 3.0 * gelu_cubic * pre_act * pre_act
    )
    return (activation, derivative)


def tap_sum(padded, kernel, tap_spacing, row_count, flipped):
    tap_count = kernel.shape[0]
    running = jnp.zeros((row_count, padded.shape[1]), jnp.float32)
    for tap_index in range(tap_count):
        source = tap_count - 1 - tap_index if flipped else tap_index
        window = padded[source * tap_spacing : source * tap_spacing + row_count].astype(jnp.float32)
        running = running + kernel[tap_index].astype(jnp.float32) * window
    return running


def tap_products(grad_pre, padded, tap_spacing, tap_count):
    row_count = grad_pre.shape[0]
    grad_wide = grad_pre.astype(jnp.float32)
    output_rows = []
    for tap_index in range(tap_count):
        window = padded[tap_index * tap_spacing : tap_index * tap_spacing + row_count].astype(
            jnp.float32
        )
        output_rows.append(jnp.sum(grad_wide * window, axis=0))
    return jnp.stack(output_rows)


def covered_at(positions, span_start, span_length):
    span_end = span_start + span_length
    within = (positions[:, None] >= span_start[None, :]) & (positions[:, None] < span_end[None, :])
    return jnp.any(within, axis=1)


def lookup(hot_rows, table_rows):
    return jnp.einsum("vt,vc->tc", hot_rows, table_rows, preferred_element_type=jnp.float32).astype(
        jnp.bfloat16
    )


def exchanged(cells, axis, bit):
    count = lax.axis_size(axis)
    return lax.ppermute(cells, axis, [(i, i ^ (1 << bit)) for i in range(count)])


def split_rows(part, bits):
    return part.reshape((2,) * bits + (part.shape[0] >> bits, part.shape[1]))


def halves_of(parts, orders, step):
    halves = []
    for part, order in zip(parts, orders):
        bit = order[step]
        dim = sorted(order[step:], reverse=True).index(bit)
        mine = (lax.axis_index("seq") >> bit) & 1
        send = lax.dynamic_index_in_dim(part, 1 - mine, dim, keepdims=False)
        keep = lax.dynamic_index_in_dim(part, mine, dim, keepdims=False)
        halves.append((keep, send))
    return halves


def swapped(halves, orders, step):
    return [
        (keep, exchanged(send, "seq", order[step])) for (keep, send), order in zip(halves, orders)
    ]


def added(keep, arrived, last):
    total = keep.astype(jnp.float32) + arrived.astype(jnp.float32)
    return total if last else total.astype(jnp.bfloat16)


def next_halves(pairs, orders, step):
    return halves_of([added(keep, arrived, False) for keep, arrived in pairs], orders, step)


def kept_with(value, pairs):
    kept = [keep for keep, arrived in pairs]
    value, kept = lax.optimization_barrier((value, kept))
    return (value, [(keep, arrived) for keep, (_, arrived) in zip(kept, pairs)])


def later_steps(pairs, orders, steps):
    for step in steps:
        pairs = swapped(next_halves(pairs, orders, step), orders, step)
    return pairs


def finished(pairs, scale):
    return jnp.concatenate([added(keep, arrived, True) for keep, arrived in pairs], axis=1) * scale


def on_device(
    base_ids, span_start, span_length, embedding, conv_kernel, mix_weight, saved_input, cotangent
):
    row_count = saved_input.shape[0]
    block_count = conv_kernel.shape[0]
    tap_count = conv_kernel.shape[1]
    taps_per_side = tap_count // 2
    vocab_rows = embedding.shape[0]
    total_rows = row_count * lax.axis_size("seq")
    grad_scale = 1.0 / math.sqrt(total_rows)
    first_row = lax.axis_index("seq") * row_count
    positions = first_row + jnp.arange(row_count, dtype=jnp.int32)
    covered = covered_at(positions, span_start, span_length)
    masked_ids = jnp.where(covered, mask_token, base_ids)
    vocab_ids = jnp.arange(vocab_rows, dtype=jnp.int32)
    one_hot = (vocab_ids[:, None] == masked_ids[None, :]).astype(jnp.bfloat16)
    bits = (lax.axis_size("seq") - 1).bit_length()
    orders = (tuple(range(bits)), (1, 0) + tuple(range(2, bits)))
    first_input = lookup(one_hot, embedding)
    steps = len(orders[0])
    halo_rows = [taps_per_side * BASE_DILATION * 2**number for number in range(block_count)]
    padded_inputs = padded_together((first_input, saved_input), halo_rows)
    upstream = jnp.where(covered[:, None], cotangent, jnp.zeros_like(cotangent))
    kernel_parts = [None] * block_count
    earlier = None
    for block_number in range(block_count - 1, -1, -1):
        tap_spacing = BASE_DILATION * 2**block_number
        reach_rows = halo_rows[block_number]
        padded_in = padded_inputs[block_number]
        kernel = conv_kernel[block_number]
        column_piece = lax.all_gather(upstream, "blk", axis=1, tiled=True)
        if earlier is not None:
            padded_in, earlier = lax.optimization_barrier((padded_in, earlier))
        pre_act = tap_sum(padded_in, kernel, tap_spacing, row_count, False)
        activation, derivative = gelu_pair(pre_act)
        act_half = activation.astype(jnp.bfloat16)
        if earlier is not None:
            halves = next_halves(earlier, orders, 1)
            earlier = swapped(halves, orders, 1)
            column_piece, earlier = kept_with(column_piece, earlier)
        grad_held = lax.dot_general(
            column_piece,
            mix_weight[block_number],
            (((1,), (1,)), ((), ())),
            preferred_element_type=jnp.float32,
        )
        grad_pre = (grad_held * derivative).astype(jnp.bfloat16)
        edges = edge_rows(grad_pre, reach_rows)
        act_half, grad_pre = lax.optimization_barrier((act_half, grad_pre))
        width = column_piece.shape[1] // len(orders)
        parts = [
            split_rows(
                lax.dot_general(
                    act_half,
                    lax.slice_in_dim(column_piece, chunk * width, (chunk + 1) * width, axis=1),
                    (((0,), (0,)), ((), ())),
                    preferred_element_type=jnp.float32,
                ).astype(jnp.bfloat16),
                steps,
            )
            for chunk in range(len(orders))
        ]
        halves = halves_of(parts, orders, 0)
        pairs = swapped(halves, orders, 0)
        edges, pairs = kept_with(edges, pairs)
        if earlier is not None:
            edges, earlier = lax.optimization_barrier((edges, earlier))
        if earlier is not None:
            earlier = later_steps(earlier, orders, range(2, 3))
        kernel_parts[block_number] = (
            tap_products(grad_pre, padded_in, tap_spacing, tap_count) * grad_scale
        )
        padded_grad = jnp.concatenate([edges[0], grad_pre, edges[1]])
        upstream = (
            upstream.astype(jnp.float32)
            + tap_sum(padded_grad, kernel, tap_spacing, row_count, True)
        ).astype(jnp.bfloat16)
        if block_number > 0:
            earlier = pairs
    embed_part = jnp.dot(one_hot, upstream, preferred_element_type=jnp.float32) * grad_scale
    sums = jnp.concatenate(kernel_parts + [embed_part])
    for step in range(steps):
        sums = sums + exchanged(sums, "seq", steps - 1 - step)
        if step < 3:
            sums, pairs, earlier = lax.optimization_barrier((sums, pairs, earlier))
            pairs = later_steps(pairs, orders, range(step + 1, step + 2 if step < 2 else steps))
            earlier = later_steps(earlier, orders, range(3, steps) if step == 0 else ())
    weight_parts = [finished(pairs, grad_scale), finished(earlier, grad_scale)]
    weight_grad = jnp.stack(weight_parts)
    kernel_grad = sums[: block_count * tap_count].reshape(block_count, tap_count, -1)
    embed_grad = sums[block_count * tap_count :]
    return (upstream, weight_grad, kernel_grad, embed_grad)


def solution(mesh):
    placed = (
        P("seq"),
        P(),
        P(),
        P(None, "blk"),
        P(None, None, "blk"),
        P(None, "blk", None),
        P("seq", "blk"),
        P("seq", "blk"),
    )
    return jax.shard_map(
        on_device,
        mesh=mesh,
        in_specs=placed,
        out_specs=(
            P("seq", "blk"),
            P(None, ("blk", "seq"), None),
            P(None, None, "blk"),
            P(None, "blk"),
        ),
        check_vma=False,
    )
```
